256 devices in a mesh: replica: 8 (over z_hi, y), fsdp: 32 (over z_lo, x, core).
Axes of the slice: x: 4, y: 4, z: 8 (z_hi: 2, z_lo: 4; z = z_hi * 4 + z_lo), core: 2. Of those that a mesh axis runs over, the one named last changes fastest.
Arguments:
- tokens: bfloat16 [8, 2, 12288, 4096], P('replica', None, 'fsdp'), may hold values from -6 to 6
- targets: bfloat16 [8, 2, 12288, 512], P('replica', None, 'fsdp'), may hold values from -6 to 6
- params: float32 [8, 4096, 512], P('replica', 'fsdp'), may hold values from -6 to 6
- first_moment: float32 [8, 4096, 512], P('replica', 'fsdp'), may hold values from -0.00061035156 to 0.00061035156
- second_moment: float32 [8, 4096, 512], P('replica', 'fsdp'), may hold values from 9.934108e-09 to 1.5894572e-07
- anchor: float32 [4096, 128], P('fsdp'), may hold values from -6 to 6
- momentum: float32 [4096, 128], P('fsdp'), may hold values from -4 to 4
- pseudo_grad: float32 [8, 4096, 128], P('replica', 'fsdp'), may hold values from -4 to 4
- fragment: int32 [1], replicated, may hold values from 0 to 3
Outputs:
- params_out: float32 [8, 4096, 512], P('replica', 'fsdp')
- anchor_out: float32 [4096, 128], P('fsdp')
- prediction: bfloat16 [8, 12288, 512], P('replica', 'fsdp')
The draws below stay inside these ranges and needn't reach their ends.
All inputs are finite; a program needn't handle non-finite values.
Results may differ from the reference program's by a relative error of at most 0.0037.
The reference program's roundings to bfloat16 on the way (of `weight` and `error`) count: a program that leaves them out, or rounds other values in their place, can miss the bound.
Values may be sent and summed in bfloat16 or wider, within the bound.
No kernel may reach another device: no remote copies, remote signals or barrier semaphores. Data moves between devices by JAX's collectives and lax.ppermute only.
A program may use at most 128 MiB of HBM per device.

```python
import math
import jax
import jax.numpy as jnp
from jax import lax

D = 4096
E = 512
HEAD = 128
STEPS = 2
STEP0 = 30
REPLICAS = 8
TOKENS = 12288
FRAGS = 4


def spiked(entries, stream_key, source, target, parts, factor):
    owner, partner = [(jnp.arange(entries.shape[dim]) // (entries.shape[dim] // parts)).reshape([-1 if axis == dim else 1 for axis in range(entries.ndim)]) for dim in (source, target)]
    chosen = jax.random.permutation(stream_key, parts)[partner]
    strong = (owner == chosen) | (owner == (partner + parts // 2) % parts)
    return jnp.where(strong, factor * entries, entries)


def block_levels(key, shape, cuts, smallest, high):
    def one(axis_at, blocks):
        draws = jax.random.uniform(jax.random.fold_in(jax.random.fold_in(key, 6), axis_at), (blocks,), jnp.float32, smallest / len(cuts), high / len(cuts))
        return jnp.repeat(jnp.exp(draws), shape[axis_at] // blocks).reshape((-1,) + (1,) * (len(shape) - axis_at - 1))

    gain = one(*cuts[0])
    for cut in cuts[1:]:
        gain = gain * one(*cut)
    return gain


def gaussian(rng, dims, spread, most, pieces=(), held_as=jnp.bfloat16):
    result = spread * jax.random.normal(rng, dims, jnp.float32)
    if pieces:
        result = result * block_levels(rng, dims, pieces, -0.22, 0.18)
    return jnp.clip(result, -most, most).astype(held_as)


def gaussian_with(stream_key, dims, spread, reach, cuts, heavy, kind=jnp.bfloat16):
    result = spread * jax.random.normal(stream_key, dims, jnp.float32)
    if cuts:
        result = result * block_levels(stream_key, dims, cuts, -0.22, 0.18)
    return jnp.clip(spiked(result, jax.random.fold_in(stream_key, 3), *heavy), -reach, reach).astype(kind)


def setup_inputs(seed: int = 0) -> dict:
    key_list = jax.random.split(jax.random.key(seed), 10)
    return {
        "tokens": gaussian_with(key_list[0], (REPLICAS, STEPS, TOKENS, D), 1.0, 6.0, ((0, 8), (2, 32)), (2, 3, 32, 2.75)),
        "targets": gaussian(key_list[1], (REPLICAS, STEPS, TOKENS, E), 1.0, 6.0, ((0, 8), (2, 32))),
        "params": gaussian(key_list[2], (REPLICAS, D, E), 1.0, 6.0, ((0, 8), (1, 32)), jnp.float32),
        "first_moment": gaussian(key_list[3], (REPLICAS, D, E), (0.3 / (D * TOKENS) ** 0.5), 0.00061035156, ((0, 8), (1, 32)), jnp.float32),
        "second_moment": jnp.clip(jnp.exp(math.log(1.5894572413799324e-07) - 2.7725887 * jax.random.uniform(key_list[4], (REPLICAS, D, E), jnp.float32) ** block_levels(key_list[4], (REPLICAS, D, E), ((0, 8), (1, 32)), -0.2, 0.2)), 9.934107758624577e-09, 1.5894572413799324e-07),
        "anchor": gaussian(key_list[5], (D, HEAD), 1.0, 6.0, ((0, 32),), jnp.float32),
        "momentum": gaussian(key_list[6], (D, HEAD), 0.3, 4.0, ((0, 32),), jnp.float32),
        "pseudo_grad": gaussian(key_list[7], (REPLICAS, D, HEAD), 0.3, 4.0, ((0, 8), (1, 32)), jnp.float32),
        "fragment": jax.random.randint(key_list[8], (1,), 0, FRAGS).astype(jnp.int32),
    }


def one_group(inputs):
    tok_steps, tgt_steps, weights, mom1, mom2 = inputs
    fwd_scale = D ** (-0.5)
    grad_scale = fwd_scale / TOKENS
    output = jnp.zeros((TOKENS, E), jnp.float32)
    for step in range(STEPS):
        weight = weights.astype(jnp.bfloat16)
        output = jnp.dot(tok_steps[step], weight, preferred_element_type=jnp.float32) * fwd_scale
        error = (output - tgt_steps[step].astype(jnp.float32)).astype(jnp.bfloat16)
        grad = jnp.dot(tok_steps[step].T, error, preferred_element_type=jnp.float32) * grad_scale
        count = STEP0 + step + 1
        mom1 = 0.9 * mom1 + 0.1 * grad
        mom2 = 0.95 * mom2 + 0.05 * grad * grad
        update = mom1 / (1.0 - 0.9 ** count) / (jnp.sqrt(mom2 / (1.0 - 0.95 ** count)) + 1e-08)
        weights = weights - 0.15 * (update + 0.1 * weights)
    return (weights, output.astype(jnp.bfloat16))

def reference(tokens, targets, params, first_moment, second_moment, anchor, momentum, pseudo_grad, fragment):
    weights, prediction = lax.map(one_group, (tokens, targets, params, first_moment, second_moment))
    mean_delta = lax.optimization_barrier(jnp.sum(pseudo_grad, axis=0)) / REPLICAS
    new_momentum = 0.9 * momentum + mean_delta
    anchor_out = anchor - 0.7 * (mean_delta + 0.9 * new_momentum)
    start = (fragment[0] * HEAD).astype(jnp.int32)
    zero = jnp.zeros((), jnp.int32)
    local = lax.dynamic_slice(weights, (zero, zero, start), (weights.shape[0], weights.shape[1], HEAD))
    mixed = 0.5 * local + 0.5 * anchor_out[None]
    params_out = lax.dynamic_update_slice(weights, mixed, (zero, zero, start))
    return (params_out, anchor_out, prediction)
```

```python
import functools

import jax
import jax.numpy as jnp
from jax import lax
from jax.experimental import pallas as pl
from jax.experimental.pallas import tpu as pltpu
from jax.sharding import PartitionSpec as P

STEPS = 2
STEP0 = 30
NZ, NX, NC = 4, 4, 2
CHIPS = NZ * NX
STREAMS = 1


def shift(value, dz=0, dx=0, dc=0):
    pairs = []
    for src in range(CHIPS * NC):
        z, x, c = src // (NX * NC), src // NC % NX, src % NC
        dst = (((z + dz) % NZ) * NX + (x + dx) % NX) * NC + (c + dc) % NC
        pairs.append((src, dst))
    return lax.ppermute(value, "fsdp", pairs)


def swap(value):
    return shift(value, dc=1)


def arrange_body(z_ref, x_ref, *refs):
    ins, outs = refs[: 2 * NX], refs[2 * NX :]
    for rx in range(NX):
        rows = ins[2 * rx].shape[0]
        outs[rx][:rows, :] = ins[2 * rx][...]
        outs[rx][rows:, :] = ins[2 * rx + 1][...]


def arrange(z, x, own, other):
    rows, width = own.shape
    block = width // CHIPS

    def spec(rx):
        return pl.BlockSpec(
            (rows, block), lambda rz, zr, xr: (0, ((zr[0] + rz) % NZ) * NX + (xr[0] + rx) % NX)
        )

    in_specs = [spec(rx) for rx in range(NX) for _ in range(2)]
    out_specs = [pl.BlockSpec((2 * rows, block), lambda rz, zr, xr: (0, rz))] * NX
    return pl.pallas_call(
        arrange_body,
        grid_spec=pltpu.PrefetchScalarGridSpec(
            num_scalar_prefetch=2, grid=(NZ,), in_specs=in_specs, out_specs=out_specs
        ),
        out_shape=[jax.ShapeDtypeStruct((2 * rows, NZ * block), own.dtype)] * NX,
        compiler_params=pltpu.CompilerParams(vmem_limit_bytes=32 * 1024 * 1024),
        cost_estimate=pl.CostEstimate(flops=0, bytes_accessed=8 * rows * width, transcendentals=0),
    )(z[None], x[None], *([own, other] * NX))


def dot(a, b):
    return jnp.dot(a, b, preferred_element_type=jnp.float32)


def dot_t(a, b):
    return lax.dot_general(a, b, (((0,), (0,)), ((), ())), preferred_element_type=jnp.float32)


def forward(segs, weight):
    stack = jnp.concatenate([weight] + [shift(weight, dz=-rz) for rz in range(1, NZ)], axis=0)
    ahead = shift(stack, dx=-1)
    behind = shift(stack, dx=1)
    half = stack.shape[0] // 2
    far_top = shift(ahead[:half], dx=-1)
    far_bot = shift(behind[half:], dx=1)
    total = dot(segs[0], stack)
    total += dot(segs[1], ahead) + dot(segs[3], behind)
    total += dot(segs[2][:, :half], far_top) + dot(segs[2][:, half:], far_bot)
    return total


def backward(segs, error):
    bf = jnp.bfloat16
    far = dot_t(segs[2], error).astype(bf)
    half = far.shape[0] // 2
    top = shift(far[:half], dx=1)
    bot = shift(far[half:], dx=-1)
    ahead = dot_t(segs[1], error)
    behind = dot_t(segs[3], error)
    ahead = jnp.concatenate([ahead[:half] + top.astype(jnp.float32), ahead[half:]], axis=0).astype(bf)
    behind = jnp.concatenate([behind[:half], behind[half:] + bot.astype(jnp.float32)], axis=0).astype(bf)
    here = dot_t(segs[0], error)
    here = here + shift(ahead, dx=1).astype(jnp.float32) + shift(behind, dx=-1).astype(jnp.float32)
    rows = here.shape[0] // NZ
    total = here[:rows]
    for rz in range(1, NZ):
        total = total + shift(here[rz * rows : (rz + 1) * rows].astype(bf), dz=rz).astype(jnp.float32)
    return total


def per_device(
    tokens, targets, params, first_moment, second_moment, anchor, momentum, pseudo_grad, fragment
):
    index = lax.axis_index("fsdp")
    group = lax.axis_size("fsdp")
    z, x, core = index // (NX * NC), index // NC % NX, index % NC
    first = core == 0
    tok_steps = tokens[0]
    tok_dev, width = tok_steps.shape[1:]
    fwd_scale = width ** (-0.5)
    grad_scale = fwd_scale / (tok_dev * group)
    cols = params.shape[2] // NC

    def mine(a):
        return jnp.where(first, a[..., :cols], a[..., cols:])

    def theirs(a):
        return jnp.where(first, a[..., cols:], a[..., :cols])

    def chip_rows(own, other):
        return jnp.where(
            first, jnp.concatenate([own, other], axis=-2), jnp.concatenate([other, own], axis=-2)
        )

    weights = chip_rows(mine(params[0]), swap(theirs(params[0])))
    segs = [arrange(z, x, tok_steps[s], swap(tok_steps[s])) for s in range(STEPS)]
    moments = jnp.concatenate([first_moment, second_moment], axis=0)
    moments = chip_rows(mine(moments), swap(theirs(moments)))
    wanted = jnp.concatenate([mine(targets[0]), swap(theirs(targets[0]))], axis=1)

    mean_delta = lax.psum(pseudo_grad[0], "replica") / lax.axis_size("replica")

    n = cols // STREAMS
    done, outputs = [], []
    for part in range(STREAMS):
        at = slice(part * n, (part + 1) * n)
        w, m, v = weights[:, at], moments[0][:, at], moments[1][:, at]
        for step in range(STEPS):
            output = forward(segs[step], w.astype(jnp.bfloat16)) * fwd_scale
            error = (output - wanted[step][:, at].astype(jnp.float32)).astype(jnp.bfloat16)
            grad = backward(segs[step], error) * grad_scale
            count = STEP0 + step + 1
            m = 0.9 * m + 0.1 * grad
            v = 0.95 * v + 0.05 * grad * grad
            update = m / (1.0 - 0.9**count) / (jnp.sqrt(v / (1.0 - 0.95**count)) + 1e-08)
            w = w - 0.15 * (update + 0.1 * w)
        done.append(w)
        outputs.append(output.astype(jnp.bfloat16))
    pred = jnp.concatenate(outputs, axis=1)
    got = swap(pred[tok_dev:])
    pred = pred[:tok_dev]
    prediction = jnp.where(
        first, jnp.concatenate([pred, got], axis=1), jnp.concatenate([got, pred], axis=1)
    )
    final = jnp.concatenate(done, axis=1)
    rows = final.shape[0] // NC
    got = swap(jnp.where(first, final[rows:], final[:rows]))
    own = jnp.where(first, final[:rows], final[rows:])
    final = jnp.where(
        first, jnp.concatenate([own, got], axis=1), jnp.concatenate([got, own], axis=1)
    )

    new_momentum = 0.9 * momentum + mean_delta
    anchor_out = anchor - 0.7 * (mean_delta + 0.9 * new_momentum)
    head = anchor.shape[1]
    heads = final.shape[1] // head
    column = lax.broadcasted_iota(jnp.int32, final.shape, 1) // head
    mixed = 0.5 * final + 0.5 * jnp.concatenate([anchor_out] * heads, axis=1)
    params_out = jnp.where(column == fragment[0], mixed, final)
    return params_out[None], anchor_out, prediction[None]


def solution(mesh):
    in_specs = (
        P("replica", None, "fsdp", None),
        P("replica", None, "fsdp", None),
        P("replica", "fsdp", None),
        P("replica", "fsdp", None),
        P("replica", "fsdp", None),
        P("fsdp", None),
        P("fsdp", None),
        P("replica", "fsdp", None),
        P(),
    )
    out_specs = (P("replica", "fsdp", None), P("fsdp", None), P("replica", "fsdp", None))
    return jax.shard_map(
        per_device, mesh=mesh, in_specs=in_specs, out_specs=out_specs, check_vma=False
    )
```

```python
import functools

import jax
import jax.numpy as jnp
from jax import lax
from jax.experimental import pallas as pl
from jax.experimental.pallas import tpu as pltpu
from jax.sharding import PartitionSpec as P

STEPS = 2
STEP0 = 30
NZ, NX, NC = 4, 4, 2
CHIPS = NZ * NX


def shift(value, dz=0, dx=0, dc=0):
    pairs = []
    for src in range(CHIPS * NC):
        z, x, c = src // (NX * NC), src // NC % NX, src % NC
        dst = (((z + dz) % NZ) * NX + (x + dx) % NX) * NC + (c + dc) % NC
        pairs.append((src, dst))
    return lax.ppermute(value, "fsdp", pairs)


def swap(value):
    return shift(value, dc=1)


def add_apart(value, apart):
    count = lax.axis_size("replica")
    return value + lax.ppermute(value, "replica", [(i, i ^ apart) for i in range(count)])


def arrange_body(z, x, own, other, *refs):
    outs, sem = refs[:NX], refs[NX]
    rows, width = own.shape
    block = width // CHIPS
    copies = []
    for rx in range(NX):
        for rz in range(NZ):
            chip = lax.rem(z[0] + rz, NZ) * NX + lax.rem(x[0] + rx, NX)
            columns = pl.ds(pl.multiple_of(chip * block, block), block)
            for half, tokens in enumerate((own, other)):
                copies.append(
                    pltpu.make_async_copy(
                        tokens.at[:, columns],
                        outs[rx].at[half * rows : (half + 1) * rows, rz * block : (rz + 1) * block],
                        sem.at[len(copies)],
                    )
                )
    for copy in copies:
        copy.start()
    for copy in copies:
        copy.wait()


def arrange(step, z, x, own, other):
    rows, width = own.shape[1:]

    def body(z, x, own, other, *refs):
        arrange_body(z, x, own.at[step], other.at[step], *refs)

    scalar = pl.BlockSpec(memory_space=pltpu.SMEM)
    return pl.pallas_call(
        body,
        in_specs=[scalar, scalar] + [pl.BlockSpec(memory_space=pltpu.HBM)] * 2,
        out_specs=[pl.BlockSpec(memory_space=pltpu.VMEM)] * NX,
        out_shape=[pltpu.VMEM((2 * rows, width // NX), own.dtype)] * NX,
        scratch_shapes=[pltpu.SemaphoreType.DMA((2 * CHIPS,))],
        compiler_params=pltpu.CompilerParams(vmem_limit_bytes=16 * 1024 * 1024),
        cost_estimate=pl.CostEstimate(flops=0, bytes_accessed=8 * rows * width, transcendentals=0),
    )(
        z[None],
        x[None],
        pltpu.with_memory_space_constraint(own, pltpu.HBM),
        pltpu.with_memory_space_constraint(other, pltpu.HBM),
    )


def dot(a, b):
    return jnp.dot(a, b, preferred_element_type=jnp.float32)


def dot_t(a, b):
    return lax.dot_general(a, b, (((0,), (0,)), ((), ())), preferred_element_type=jnp.float32)


def after(value, other):
    return lax.optimization_barrier((value, other))[0]


def gather_z(weight):
    return [weight] + [shift(weight, dz=-rz) for rz in range(1, NZ)]


def forward(segs, stack):
    ahead = shift(stack, dx=-1)
    behind = shift(stack, dx=1)
    half = stack.shape[0] // 2
    far_top = shift(ahead[:half], dx=-1)
    far_bot = shift(behind[half:], dx=1)
    total = dot(segs[0], stack)
    total += dot(segs[1], ahead) + dot(segs[3], behind)
    total += dot(segs[2][:, :half], far_top) + dot(segs[2][:, half:], far_bot)
    return total


def backward(segs, error, beside):
    bf, f32 = jnp.bfloat16, jnp.float32
    half = segs[2].shape[1] // 2
    rows = segs[2].shape[1] // NZ
    top = shift(dot_t(segs[2][:, :half], error).astype(bf), dx=1)
    bot = shift(dot_t(segs[2][:, half:], error).astype(bf), dx=-1)
    ahead, behind = lax.optimization_barrier((dot_t(segs[1], error), dot_t(segs[3], error)))
    ahead_own = (ahead[:rows] + top[:rows].astype(f32)).astype(bf)
    ahead = (ahead[rows:] + jnp.pad(top[rows:], ((0, half), (0, 0))).astype(f32)).astype(bf)
    behind_own = behind[:rows].astype(bf)
    behind = (behind[rows:] + jnp.pad(bot, ((half - rows, 0), (0, 0))).astype(f32)).astype(bf)
    ahead, behind = shift(ahead, dx=1), shift(behind, dx=-1)
    ahead_own, behind_own = shift(ahead_own, dx=1), shift(behind_own, dx=-1)
    here, beside = lax.optimization_barrier((dot_t(segs[0], error), beside))
    column = (here[rows:] + ahead.astype(f32) + behind.astype(f32)).astype(bf)
    got = [shift(column[(rz - 1) * rows : rz * rows], dz=rz) for rz in range(1, NZ)]
    total = here[:rows] + ahead_own.astype(f32) + behind_own.astype(f32)
    for value in got:
        total = total + value.astype(f32)
    return total, beside


def per_device(
    tokens, targets, params, first_moment, second_moment, anchor, momentum, pseudo_grad, fragment
):
    index = lax.axis_index("fsdp")
    group = lax.axis_size("fsdp")
    z, x, core = index // (NX * NC), index // NC % NX, index % NC
    first = core == 0
    tok_steps = tokens[0]
    tok_dev, width = tok_steps.shape[1:]
    fwd_scale = width ** (-0.5)
    grad_scale = fwd_scale / (tok_dev * group)
    cols = params.shape[2] // NC

    def mine(a):
        return jnp.where(first, a[..., :cols], a[..., cols:])

    def theirs(a):
        return jnp.where(first, a[..., cols:], a[..., :cols])

    def chip_rows(own, other):
        return jnp.where(
            first, jnp.concatenate([own, other], axis=-2), jnp.concatenate([other, own], axis=-2)
        )

    weights = chip_rows(mine(params[0]), swap(theirs(params[0])))
    w16 = weights.astype(jnp.bfloat16)
    swapped = swap(after(tok_steps, w16))
    stack = jnp.concatenate(gather_z(w16), axis=0)
    stack, swapped, late_m, late_v, late_targets, group_sum = lax.optimization_barrier(
        (stack, swapped, first_moment, second_moment, targets[0], pseudo_grad[0])
    )
    segs = [arrange(s, z, x, tok_steps, swapped) for s in range(STEPS)]
    moments = jnp.concatenate([late_m, late_v], axis=0)
    m, v = chip_rows(mine(moments), swap(theirs(moments)))
    wanted = jnp.concatenate([mine(late_targets), swap(theirs(late_targets))], axis=1)

    group_sum = add_apart(group_sum, 2)
    for step in range(STEPS):
        output = forward(segs[step], stack) * fwd_scale
        error = (output - wanted[step].astype(jnp.float32)).astype(jnp.bfloat16)
        if step == 0:
            error, group_sum = lax.optimization_barrier((error, group_sum))
            group_sum = add_apart(group_sum, 1)
            grad, group_sum = backward(segs[step], error, group_sum)
        else:
            group_sum = add_apart(after(group_sum, error), 4)
            grad, group_sum = backward(segs[step], error, group_sum)
        grad = grad * grad_scale
        count = STEP0 + step + 1
        m = 0.9 * m + 0.1 * grad
        v = 0.95 * v + 0.05 * grad * grad
        update = m / (1.0 - 0.9**count) / (jnp.sqrt(v / (1.0 - 0.95**count)) + 1e-08)
        weights = weights - 0.15 * (update + 0.1 * weights)
        if step < STEPS - 1:
            stack = jnp.concatenate(gather_z(weights.astype(jnp.bfloat16)), axis=0)
    pred = output.astype(jnp.bfloat16)
    got = swap(pred[tok_dev:])
    pred = pred[:tok_dev]
    prediction = jnp.where(
        first, jnp.concatenate([pred, got], axis=1), jnp.concatenate([got, pred], axis=1)
    )
    rows = weights.shape[0] // NC
    got = swap(jnp.where(first, weights[rows:], weights[:rows]))
    own = jnp.where(first, weights[:rows], weights[rows:])
    final = jnp.where(
        first, jnp.concatenate([own, got], axis=1), jnp.concatenate([got, own], axis=1)
    )

    mean_delta = group_sum / lax.axis_size("replica")
    new_momentum = 0.9 * momentum + mean_delta
    anchor_out = anchor - 0.7 * (mean_delta + 0.9 * new_momentum)
    head = anchor.shape[1]
    heads = final.shape[1] // head
    column = lax.broadcasted_iota(jnp.int32, final.shape, 1) // head
    mixed = 0.5 * final + 0.5 * jnp.concatenate([anchor_out] * heads, axis=1)
    params_out = jnp.where(column == fragment[0], mixed, final)
    return params_out[None], anchor_out, prediction[None]


def solution(mesh):
    in_specs = (
        P("replica", None, "fsdp", None),
        P("replica", None, "fsdp", None),
        P("replica", "fsdp", None),
        P("replica", "fsdp", None),
        P("replica", "fsdp", None),
        P("fsdp", None),
        P("fsdp", None),
        P("replica", "fsdp", None),
        P(),
    )
    out_specs = (P("replica", "fsdp", None), P("fsdp", None), P("replica", "fsdp", None))
    return jax.shard_map(
        per_device, mesh=mesh, in_specs=in_specs, out_specs=out_specs, check_vma=False
    )
```

```python
import functools

import jax
import jax.numpy as jnp
from jax import lax
from jax.experimental import pallas as pl
from jax.experimental.pallas import tpu as pltpu
from jax.sharding import PartitionSpec as P

STEPS = 2
STEP0 = 30
NZ, NX, NC = 4, 4, 2
CHIPS = NZ * NX


def shift(value, dz=0, dx=0, dc=0):
    pairs = []
    for src in range(CHIPS * NC):
        z, x, c = src // (NX * NC), src // NC % NX, src % NC
        dst = (((z + dz) % NZ) * NX + (x + dx) % NX) * NC + (c + dc) % NC
        pairs.append((src, dst))
    return lax.ppermute(value, "fsdp", pairs)


def swap(value):
    return shift(value, dc=1)


def add_apart(value, apart):
    count = lax.axis_size("replica")
    return value + lax.ppermute(value, "replica", [(i, i ^ apart) for i in range(count)])


def arrange_body(z, x, own, other, *refs):
    outs, sem = refs[:NX], refs[NX]
    rows, width = own.shape
    block = width // CHIPS
    copies = []
    for rx in range(NX):
        for rz in range(NZ):
            chip = lax.rem(z[0] + rz, NZ) * NX + lax.rem(x[0] + rx, NX)
            columns = pl.ds(pl.multiple_of(chip * block, block), block)
            for half, tokens in enumerate((own, other)):
                copies.append(
                    pltpu.make_async_copy(
                        tokens.at[:, columns],
                        outs[rx].at[half * rows : (half + 1) * rows, rz * block : (rz + 1) * block],
                        sem.at[len(copies)],
                    )
                )
    for copy in copies:
        copy.start()
    for copy in copies:
        copy.wait()


def arrange(step, z, x, own, other):
    rows, width = own.shape[1:]

    def body(z, x, own, other, *refs):
        arrange_body(z, x, own.at[step], other.at[step], *refs)

    scalar = pl.BlockSpec(memory_space=pltpu.SMEM)
    return pl.pallas_call(
        body,
        in_specs=[scalar, scalar] + [pl.BlockSpec(memory_space=pltpu.HBM)] * 2,
        out_specs=[pl.BlockSpec(memory_space=pltpu.VMEM)] * NX,
        out_shape=[pltpu.VMEM((2 * rows, width // NX), own.dtype)] * NX,
        scratch_shapes=[pltpu.SemaphoreType.DMA((2 * CHIPS,))],
        compiler_params=pltpu.CompilerParams(vmem_limit_bytes=16 * 1024 * 1024),
        cost_estimate=pl.CostEstimate(flops=0, bytes_accessed=8 * rows * width, transcendentals=0),
    )(
        z[None],
        x[None],
        pltpu.with_memory_space_constraint(own, pltpu.HBM),
        pltpu.with_memory_space_constraint(other, pltpu.HBM),
    )


def dot(a, b):
    return jnp.dot(a, b, preferred_element_type=jnp.float32)


def dot_t(a, b):
    return lax.dot_general(a, b, (((0,), (0,)), ((), ())), preferred_element_type=jnp.float32)


def after(value, other):
    return lax.optimization_barrier((value, other))[0]


def gather_z(weight):
    return [weight] + [shift(weight, dz=-rz) for rz in range(1, NZ)]


def forward(segs, stack):
    ahead = shift(stack, dx=-1)
    behind = shift(stack, dx=1)
    half = stack.shape[0] // 2
    far_top = shift(ahead[:half], dx=-1)
    far_bot = shift(behind[half:], dx=1)
    total = dot(segs[0], stack)
    total += dot(segs[1], ahead) + dot(segs[3], behind)
    total += dot(segs[2][:, :half], far_top) + dot(segs[2][:, half:], far_bot)
    return total


def backward(segs, error, beside):
    bf, f32 = jnp.bfloat16, jnp.float32
    half = segs[2].shape[1] // 2
    rows = segs[2].shape[1] // NZ
    top = shift(dot_t(segs[2][:, :half], error).astype(bf), dx=1)
    bot = shift(dot_t(segs[2][:, half:], error).astype(bf), dx=-1)
    ahead, behind = lax.optimization_barrier((dot_t(segs[1], error), dot_t(segs[3], error)))
    ahead_own = (ahead[:rows] + top[:rows].astype(f32)).astype(bf)
    ahead = (ahead[rows:] + jnp.pad(top[rows:], ((0, half), (0, 0))).astype(f32)).astype(bf)
    behind_own = behind[:rows].astype(bf)
    behind = (behind[rows:] + jnp.pad(bot, ((half - rows, 0), (0, 0))).astype(f32)).astype(bf)
    ahead, behind = shift(ahead, dx=1), shift(behind, dx=-1)
    here, beside = lax.optimization_barrier((dot_t(segs[0], error), beside))
    column = (here[rows:] + ahead.astype(f32) + behind.astype(f32)).astype(bf)
    ahead_own, behind_own, column = lax.optimization_barrier((ahead_own, behind_own, column))
    ahead_own, behind_own = shift(ahead_own, dx=1), shift(behind_own, dx=-1)
    got = [shift(column[(rz - 1) * rows : rz * rows], dz=rz) for rz in range(1, NZ)]
    total = here[:rows] + ahead_own.astype(f32) + behind_own.astype(f32)
    for value in got:
        total = total + value.astype(f32)
    return total, beside


def per_device(
    tokens, targets, params, first_moment, second_moment, anchor, momentum, pseudo_grad, fragment
):
    index = lax.axis_index("fsdp")
    group = lax.axis_size("fsdp")
    z, x, core = index // (NX * NC), index // NC % NX, index % NC
    first = core == 0
    tok_steps = tokens[0]
    tok_dev, width = tok_steps.shape[1:]
    fwd_scale = width ** (-0.5)
    grad_scale = fwd_scale / (tok_dev * group)
    cols = params.shape[2] // NC

    def mine(a):
        return jnp.where(first, a[..., :cols], a[..., cols:])

    def theirs(a):
        return jnp.where(first, a[..., cols:], a[..., :cols])

    def chip_rows(own, other):
        return jnp.where(
            first, jnp.concatenate([own, other], axis=-2), jnp.concatenate([other, own], axis=-2)
        )

    weights = chip_rows(mine(params[0]), swap(theirs(params[0])))
    w16 = weights.astype(jnp.bfloat16)
    swapped = swap(after(tok_steps, w16))
    stack = jnp.concatenate(gather_z(w16), axis=0)
    stack, swapped, late_m, late_v, late_targets, group_sum = lax.optimization_barrier(
        (stack, swapped, first_moment, second_moment, targets[0], pseudo_grad[0])
    )
    segs = [arrange(s, z, x, tok_steps, swapped) for s in range(STEPS)]
    moments = jnp.concatenate([late_m, late_v], axis=0)
    m, v = chip_rows(mine(moments), swap(theirs(moments)))
    wanted = jnp.concatenate([mine(late_targets), swap(theirs(late_targets))], axis=1)

    group_sum = add_apart(group_sum, 2)
    for step in range(STEPS):
        output = forward(segs[step], stack) * fwd_scale
        error = (output - wanted[step].astype(jnp.float32)).astype(jnp.bfloat16)
        if step == 0:
            error, group_sum = lax.optimization_barrier((error, group_sum))
            group_sum = add_apart(group_sum, 1)
            grad, group_sum = backward(segs[step], error, group_sum)
        else:
            group_sum = add_apart(after(group_sum, error), 4)
            grad, group_sum = backward(segs[step], error, group_sum)
        grad = grad * grad_scale
        count = STEP0 + step + 1
        m = 0.9 * m + 0.1 * grad
        v = 0.95 * v + 0.05 * grad * grad
        update = m / (1.0 - 0.9**count) / (jnp.sqrt(v / (1.0 - 0.95**count)) + 1e-08)
        weights = weights - 0.15 * (update + 0.1 * weights)
        if step < STEPS - 1:
            stack = jnp.concatenate(gather_z(weights.astype(jnp.bfloat16)), axis=0)
    pred = output.astype(jnp.bfloat16)
    got = swap(pred[tok_dev:])
    pred = pred[:tok_dev]
    prediction = jnp.where(
        first, jnp.concatenate([pred, got], axis=1), jnp.concatenate([got, pred], axis=1)
    )
    rows = weights.shape[0] // NC
    got = swap(jnp.where(first, weights[rows:], weights[:rows]))
    own = jnp.where(first, weights[:rows], weights[rows:])
    final = jnp.where(
        first, jnp.concatenate([own, got], axis=1), jnp.concatenate([got, own], axis=1)
    )

    mean_delta = group_sum / lax.axis_size("replica")
    new_momentum = 0.9 * momentum + mean_delta
    anchor_out = anchor - 0.7 * (mean_delta + 0.9 * new_momentum)
    head = anchor.shape[1]
    heads = final.shape[1] // head
    column = lax.broadcasted_iota(jnp.int32, final.shape, 1) // head
    mixed = 0.5 * final + 0.5 * jnp.concatenate([anchor_out] * heads, axis=1)
    params_out = jnp.where(column == fragment[0], mixed, final)
    return params_out[None], anchor_out, prediction[None]


def solution(mesh):
    in_specs = (
        P("replica", None, "fsdp", None),
        P("replica", None, "fsdp", None),
        P("replica", "fsdp", None),
        P("replica", "fsdp", None),
        P("replica", "fsdp", None),
        P("fsdp", None),
        P("fsdp", None),
        P("replica", "fsdp", None),
        P(),
    )
    out_specs = (P("replica", "fsdp", None), P("fsdp", None), P("replica", "fsdp", None))
    return jax.shard_map(
        per_device, mesh=mesh, in_specs=in_specs, out_specs=out_specs, check_vma=False
    )
```
